32 devices in a mesh: dp: 8 (over z, x), tensor: 4 (over y, core).
Axes of the slice: x: 2, y: 2, z: 4, core: 2. Of those that a mesh axis runs over, the one named last changes fastest.
Arguments:
- attn_out: bfloat16 [8192, 8192], P('dp', 'tensor'), may hold values from -8 to 8, as said below
- grad_out: bfloat16 [8192, 256], P('dp'), may hold values from -1.0080408 to 1.0080408, as said below
- grad_acc: float32 [256, 8192], P('dp', 'tensor'), may hold values from -1060 to 1060, as said below
- master_weight: float32 [256, 8192], P('dp', 'tensor'), may hold values from -60 to 60, as said below
- moment_m: float32 [256, 8192], P('dp', 'tensor'), may hold values from -4 to 4
- moment_v: float32 [256, 8192], P('dp', 'tensor'), may hold values from 0.001 to 0.01
Outputs:
- moment_new: float32 [256, 8192], P('dp', 'tensor')
- second_new: float32 [256, 8192], P('dp', 'tensor')
- scaled_step: float32 [256, 8192], P('dp', 'tensor')
The draws below stay inside these ranges and needn't reach their ends.
Inputs may be any that keep to these rules, and one draw needn't show every extreme that they name: `attn_out`: finite values. `grad_out`: finite values. `grad_acc`: finite values. `master_weight`: finite values.
All inputs are finite; a program needn't handle non-finite values.
Results may differ from the reference program's by a relative error of at most 0.0003.
Values sent between devices are 32-bit elements; how exact they have to be, the bound alone decides.
A program may use at most 128 MiB of HBM per device.

```python
import math
import jax
import jax.numpy as jnp
from jax import lax

ROWS_DEV = 8
TOK_DEV = 1024
TOKENS = 8192
IN_FEATURES = 8192
OUT_ROWS = 256
N_TENSOR = 4


def loguniform_draw(key, count, low, high):
    return jnp.exp(jax.random.uniform(key, (count,), jnp.float32, math.log(low), math.log(high)))


def shared_factors(key):
    subkeys = jax.random.split(jax.random.fold_in(key, 101), 4)
    token_sign = jnp.where(jax.random.bernoulli(subkeys[0], 0.5, (TOKENS,)), 1.0, -1.0).astype(jnp.float32)
    row_dir = jnp.clip(jax.random.normal(subkeys[1], (OUT_ROWS,), jnp.float32), -4.0, 4.0)
    col_dir = jnp.clip(jax.random.normal(subkeys[2], (IN_FEATURES,), jnp.float32), -4.0, 4.0)
    pairing = jax.random.permutation(subkeys[3], TOKENS // TOK_DEV)
    return (token_sign, row_dir, col_dir, pairing)


def draw_attn_out(key, part):
    token_sign, row_dir, col_dir, pairing = shared_factors(key)
    noise_key = jax.random.fold_in(key, 31)
    noise = jnp.clip(jax.random.normal(noise_key, (TOKENS, IN_FEATURES), jnp.float32), -6.0, 6.0)
    strength = 0.5
    return (noise + strength * token_sign[:, None] * col_dir[None, :]).astype(jnp.bfloat16)


def draw_grad_out(key, part):
    token_sign, row_dir, col_dir, pairing = shared_factors(key)
    noise_key = jax.random.fold_in(key, 37)
    sigma = 5.0 / math.sqrt(TOKENS)
    noise = jnp.clip(jax.random.normal(noise_key, (TOKENS, OUT_ROWS), jnp.float32), -6.0, 6.0)
    token_block = jnp.arange(TOKENS) // TOK_DEV
    row_block = jnp.arange(OUT_ROWS) // (ROWS_DEV * N_TENSOR)
    paired = pairing[token_block][:, None] == row_block[None, :]
    factor = jnp.where(paired, 3.0, 1.0).astype(jnp.float32)
    coherent = 28.0 / TOKENS * token_sign[:, None] * row_dir[None, :]
    return (sigma * noise * factor + coherent).astype(jnp.bfloat16)


def draw_grad_acc(key, part):
    subkeys = jax.random.split(jax.random.fold_in(key, 11), 3)
    row_ramp = 3.0 ** (jnp.arange(OUT_ROWS, dtype=jnp.float32) / max(OUT_ROWS - 1, 1))
    base_values = jnp.clip(jax.random.normal(subkeys[0], (OUT_ROWS, IN_FEATURES), jnp.float32), -6.0, 6.0)
    row_factor = loguniform_draw(subkeys[1], OUT_ROWS, 1.0, 4.0)
    column_factor = loguniform_draw(subkeys[2], IN_FEATURES, 1.0, 10.0)
    values = base_values * (row_ramp * row_factor)[:, None] * column_factor[None, :]
    return values.astype(jnp.float32)


def draw_master_weight(key, part):
    subkeys = jax.random.split(jax.random.fold_in(key, 23), 3)
    base_values = jnp.clip(jax.random.normal(subkeys[0], (OUT_ROWS, IN_FEATURES), jnp.float32), -6.0, 6.0)
    row_factor = loguniform_draw(subkeys[1], OUT_ROWS, 1.0, 10.0)
    column_factor = loguniform_draw(subkeys[2], IN_FEATURES, 1.0, 10.0)
    return (0.1 * base_values * row_factor[:, None] * column_factor[None, :]).astype(jnp.float32)


def shard_levels(key, dims, pieces, least, top_value):
    level = 1.0
    for axis_at, parts in pieces:
        draws = jax.random.uniform(jax.random.fold_in(jax.random.fold_in(key, 6), axis_at), (parts,), jnp.float32, least / len(pieces), top_value / len(pieces))
        level = level * jnp.repeat(jnp.exp(draws), dims[axis_at] // parts).reshape((-1,) + (1,) * (len(dims) - 1 - axis_at))
    return level


def gaussian(own_key, shape, deviation, limit, pieces=(), kind=jnp.bfloat16):
    factor_of = shard_levels(own_key, shape, pieces, -0.22, 0.18) if pieces else 1.0
    result = jax.random.normal(own_key, shape, jnp.float32) * deviation * factor_of
    return jnp.minimum(jnp.maximum(result, -limit), limit).astype(kind)


def setup_inputs(seed: int = 0) -> dict:
    splits = jax.random.split(jax.random.key(seed), 7)
    attn_out = draw_attn_out(jax.random.fold_in(splits[6], 71), 0)
    grad_out = draw_grad_out(jax.random.fold_in(splits[6], 71), 0)
    grad_acc = draw_grad_acc(jax.random.fold_in(splits[6], 71), 0)
    master_weight = draw_master_weight(jax.random.fold_in(splits[6], 71), 0)
    moment_m = gaussian(splits[4], (OUT_ROWS, IN_FEATURES), 0.3, 4.0, ((0, 8), (1, 4)), jnp.float32)
    moment_v = jnp.clip(jnp.exp(math.log(0.01) - 2.30258502 * jax.random.uniform(splits[5], (OUT_ROWS, IN_FEATURES), jnp.float32) ** shard_levels(splits[5], (OUT_ROWS, IN_FEATURES), ((0, 8), (1, 4)), -0.2, 0.2)), 0.001, 0.01)
    return dict(attn_out=attn_out, grad_out=grad_out, grad_acc=grad_acc, master_weight=master_weight, moment_m=moment_m, moment_v=moment_v)


beta_first = 0.9
beta_second = 0.999
weight_decay = 0.01
epsilon = 1e-06

def lamb_moments(gradient, divisor, weight, moment, second):
    clipped = gradient / divisor
    moment_new = beta_first * moment + (1.0 - beta_first) * clipped
    second_new = beta_second * second + (1.0 - beta_second) * clipped * clipped
    update = moment_new / (jnp.sqrt(second_new) + epsilon) + weight_decay * weight
    return (moment_new, second_new, update)

def reference(attn_out, grad_out, grad_acc, master_weight, moment_m, moment_v):
    batch_grad = lax.dot_general(grad_out, attn_out, (((0,), (0,)), ((), ())), preferred_element_type=jnp.float32)
    gradient = grad_acc + batch_grad
    grad_rms = jnp.sqrt(jnp.sum(gradient * gradient) / (OUT_ROWS * IN_FEATURES) + epsilon)
    moment_new, second_new, update = lamb_moments(gradient, grad_rms, master_weight, moment_m, moment_v)
    weight_norm = jnp.sqrt(lax.optimization_barrier(jnp.sum(master_weight * master_weight, axis=1, keepdims=True)))
    update_norm = jnp.sqrt(lax.optimization_barrier(jnp.sum(update * update, axis=1, keepdims=True)))
    scaled_step = weight_norm / (update_norm + epsilon) * update
    return (moment_new, second_new, scaled_step)
```

```python
import functools

import jax
import jax.numpy as jnp
from jax import lax
from jax.experimental import pallas as pl
from jax.experimental.pallas import tpu as pltpu
from jax.sharding import PartitionSpec as P

beta_first = 0.9
beta_second = 0.999
weight_decay = 0.01
epsilon = 1e-06

MESH = pl.DeviceIdType.MESH
CHUNKS = 4
AHEAD = 4
LANES = 128
MAX_LINE = 4


def lamb_moments(gradient, divisor, weight, moment, second):
    clipped = gradient / divisor
    moment_new = beta_first * moment + (1.0 - beta_first) * clipped
    second_new = beta_second * second + (1.0 - beta_second) * clipped * clipped
    update = moment_new / (jnp.sqrt(second_new) + epsilon) + weight_decay * weight
    return (moment_new, second_new, update)


def block_order(at, line):
    right = list(range(line - 1, at, -1))
    left = list(range(0, at))
    order = []
    while right or left:
        group = []
        if right and len(right) >= len(left):
            group.append(right.pop(0))
            if left and len(left) > len(right):
                group.append(left.pop(0))
        else:
            group.append(left.pop(0))
            if right and len(right) > len(left):
                group.append(right.pop(0))
        order += [(place, chunk) for chunk in range(CHUNKS) for place in group]
    return order + [(at, chunk) for chunk in range(CHUNKS)]


def lane_sums(values):
    total = values[:, :LANES]
    for at in range(LANES, values.shape[1], LANES):
        total = total + values[:, at : at + LANES]
    return total


def row_groups(values):
    total = values[:8]
    for at in range(8, values.shape[0], 8):
        total = total + values[at : at + 8]
    return total


def lamb_kernel(
    n_dp, n_tensor, entry_count,
    attn, grad_out, grad_acc, weight, moment, second,
    moment_out, second_out, step_out,
    a_buf, g_buf, gt_buf, part, pair_in, from_left, from_right,
    acc_buf, w_buf, m_buf, v_buf, grad_buf, mo_buf, so_buf, st_buf,
    wsum, usum, esum, tsum,
    load_sem, out_sem,
    pair_send, pair_recv, right_send, right_recv, left_send, left_recv,
    w_send, w_recv, u_send, u_recv, e_send, e_recv, t_send, t_recv,
):
    line = n_dp // 2
    dp = lax.axis_index("dp")
    tensor = lax.axis_index("tensor")
    place, side = dp // 2, dp % 2
    width = part.shape[3]

    loads = [pltpu.make_async_copy(grad_out, g_buf, load_sem.at[0])]
    for c in range(CHUNKS):
        loads.append(
            pltpu.make_async_copy(attn.at[:, pl.ds(c * width, width)], a_buf.at[c], load_sem.at[1 + c])
        )
    for i, (src, dst) in enumerate(((weight, w_buf), (grad_acc, acc_buf), (moment, m_buf), (second, v_buf))):
        loads.append(pltpu.make_async_copy(src, dst, load_sem.at[1 + CHUNKS + i]))
    for copy in loads:
        copy.start()

    dp_peer = [lax.rem(dp + k, n_dp) for k in range(n_dp)]
    tensor_peer = [lax.rem(tensor + k, n_tensor) for k in range(n_tensor)]

    barrier = pltpu.get_barrier_semaphore()
    for k in range(1, n_dp):
        pl.semaphore_signal(barrier, inc=1, device_id=(dp_peer[k], tensor), device_id_type=MESH)
    for k in range(1, n_tensor):
        pl.semaphore_signal(barrier, inc=1, device_id=(dp, tensor_peer[k]), device_id_type=MESH)

    def pair_copy(item):
        to, c = item
        i = to * CHUNKS + c
        return pltpu.make_async_remote_copy(
            src_ref=part.at[2 * to + (1 - side), c], dst_ref=pair_in.at[to, c],
            send_sem=pair_send.at[i], recv_sem=pair_recv.at[i],
            device_id=(2 * place + (1 - side), tensor), device_id_type=MESH,
        )

    def line_copy(item, step):
        to, c = item
        i = to * CHUNKS + c
        into, send, recv = (from_left, right_send, right_recv) if step > 0 else (from_right, left_send, left_recv)
        return pltpu.make_async_remote_copy(
            src_ref=part.at[2 * to + side, c], dst_ref=into.at[to, c],
            send_sem=send.at[i], recv_sem=recv.at[i],
            device_id=(dp + 2 * step, tensor), device_id_type=MESH,
        )

    def tensor_copy(k, src, dst, send, recv):
        return pltpu.make_async_remote_copy(
            src_ref=src, dst_ref=dst.at[k], send_sem=send.at[k], recv_sem=recv.at[k],
            device_id=(dp, tensor_peer[k]), device_id_type=MESH,
        )

    def dp_copy(k, src, dst, send, recv):
        return pltpu.make_async_remote_copy(
            src_ref=src, dst_ref=dst.at[k], send_sem=send.at[k], recv_sem=recv.at[k],
            device_id=(dp_peer[k], tensor), device_id_type=MESH,
        )

    loads[0].wait()
    gt_buf[...] = g_buf[...].T

    orders = [block_order(at, line) for at in range(line)]
    for c in range(CHUNKS):
        loads[1 + c].wait()
        product = jnp.dot(gt_buf[...], a_buf[c], preferred_element_type=jnp.float32)
        part[:, c] = product.reshape(n_dp, product.shape[0] // n_dp, width)
        if c == 0:
            pl.semaphore_wait(barrier, n_dp + n_tensor - 2)
        for at in range(line):
            @pl.when(place == at)
            def _(at=at, c=c):
                for item in orders[at][:AHEAD]:
                    if item[1] == c:
                        pair_copy(item).start()

    loads[1 + CHUNKS].wait()
    wsum[0] = lane_sums(jnp.square(w_buf[...]))
    w_copies = [tensor_copy(k, wsum.at[0], wsum, w_send, w_recv) for k in range(1, n_tensor)]
    for copy in w_copies:
        copy.start()
    for i in range(1, 4):
        loads[1 + CHUNKS + i].wait()

    for at in range(line):
        @pl.when(place == at)
        def _(at=at):
            order = orders[at]
            energy = jnp.zeros((8, LANES), jnp.float32)
            for i, item in enumerate(order):
                to, c = item
                pair_copy(item).wait_recv()
                if i + AHEAD < len(order):
                    pair_copy(order[i + AHEAD]).start()
                total = part[2 * to + side, c] + pair_in[to, c]
                if at > 0 and to >= at:
                    line_copy(item, 1).wait_recv()
                    total = total + from_left[to, c]
                if at < line - 1 and to <= at:
                    line_copy(item, -1).wait_recv()
                    total = total + from_right[to, c]
                if to != at:
                    part[2 * to + side, c] = total
                    line_copy(item, 1 if to > at else -1).start()
                else:
                    total = total + acc_buf[:, c * width : (c + 1) * width]
                    grad_buf[:, c * width : (c + 1) * width] = total
                    energy = energy + row_groups(lane_sums(jnp.square(total)))
            tsum[0] = energy

    t_copies = [tensor_copy(k, tsum.at[0], tsum, t_send, t_recv) for k in range(1, n_tensor)]
    for copy in t_copies:
        copy.start()
    energy = tsum[0]
    for k, copy in enumerate(t_copies):
        copy.wait_recv()
        energy = energy + tsum[k + 1]
    esum[0] = energy
    e_copies = [dp_copy(k, esum.at[0], esum, e_send, e_recv) for k in range(1, n_dp)]
    for copy in e_copies:
        copy.start()
    for k, copy in enumerate(e_copies):
        copy.wait_recv()
        energy = energy + esum[k + 1]
    mean_square = jnp.sum(energy, keepdims=True) * (1.0 / entry_count)
    divisor = jnp.sqrt(mean_square + epsilon)

    moment_new, second_new, update = lamb_moments(grad_buf[...], divisor, w_buf[...], m_buf[...], v_buf[...])
    st_buf[...] = update
    usum[0] = lane_sums(update * update)
    u_copies = [tensor_copy(k, usum.at[0], usum, u_send, u_recv) for k in range(1, n_tensor)]
    for copy in u_copies:
        copy.start()
    mo_buf[...] = moment_new
    so_buf[...] = second_new
    outs = [
        pltpu.make_async_copy(mo_buf, moment_out, out_sem.at[0]),
        pltpu.make_async_copy(so_buf, second_out, out_sem.at[1]),
        pltpu.make_async_copy(st_buf, step_out, out_sem.at[2]),
    ]
    outs[0].start()
    outs[1].start()
    weight_square = wsum[0]
    for k, copy in enumerate(w_copies):
        copy.wait_recv()
        weight_square = weight_square + wsum[k + 1]
    weight_norm = jnp.sqrt(jnp.sum(weight_square, axis=1, keepdims=True))
    update_square = usum[0]
    for k, copy in enumerate(u_copies):
        copy.wait_recv()
        update_square = update_square + usum[k + 1]
    update_norm = jnp.sqrt(jnp.sum(update_square, axis=1, keepdims=True))
    st_buf[...] = weight_norm / (update_norm + epsilon) * st_buf[...]
    outs[2].start()

    for copy in w_copies + t_copies + e_copies + u_copies:
        copy.wait_send()
    for at in range(line):
        @pl.when(place == at)
        def _(at=at):
            for item in orders[at]:
                pair_copy(item).wait_send()
                if item[0] != at:
                    line_copy(item, 1 if item[0] > at else -1).wait_send()
    for copy in outs:
        copy.wait()


def kernel_shards(n_dp, n_tensor, attn_out, grad_out, grad_acc, master_weight, moment_m, moment_v):
    tokens, columns = attn_out.shape
    rows_all = grad_out.shape[1]
    rows = rows_all // n_dp
    line = n_dp // 2
    width = columns // CHUNKS
    f32 = jnp.float32
    items = line * CHUNKS
    dma = pltpu.SemaphoreType.DMA
    whole = lambda: pltpu.VMEM((rows, columns), f32)
    out = jax.ShapeDtypeStruct((rows, columns), f32)
    return pl.pallas_call(
        functools.partial(lamb_kernel, n_dp, n_tensor, rows_all * columns * n_tensor),
        out_shape=(out, out, out),
        in_specs=[pl.BlockSpec(memory_space=pl.ANY)] * 6,
        out_specs=[pl.BlockSpec(memory_space=pl.ANY)] * 3,
        scratch_shapes=[
            pltpu.VMEM((CHUNKS, tokens, width), jnp.bfloat16),
            pltpu.VMEM((tokens, rows_all), jnp.bfloat16),
            pltpu.VMEM((rows_all, tokens), jnp.bfloat16),
            pltpu.VMEM((n_dp, CHUNKS, rows, width), f32),
            pltpu.VMEM((line, CHUNKS, rows, width), f32),
            pltpu.VMEM((line, CHUNKS, rows, width), f32),
            pltpu.VMEM((line, CHUNKS, rows, width), f32),
            whole(), whole(), whole(), whole(), whole(), whole(), whole(), whole(),
            pltpu.VMEM((n_tensor, rows, LANES), f32),
            pltpu.VMEM((n_tensor, rows, LANES), f32),
            pltpu.VMEM((n_dp, 8, LANES), f32),
            pltpu.VMEM((n_tensor, 8, LANES), f32),
            dma((CHUNKS + 5,)), dma((3,)),
            dma((items,)), dma((items,)), dma((items,)), dma((items,)), dma((items,)), dma((items,)),
            dma((n_tensor,)), dma((n_tensor,)), dma((n_tensor,)), dma((n_tensor,)),
            dma((n_dp,)), dma((n_dp,)), dma((n_tensor,)), dma((n_tensor,)),
        ],
        compiler_params=pltpu.CompilerParams(
            collective_id=0, has_side_effects=True, vmem_limit_bytes=40 * 2**20
        ),
        name="lamb_step",
    )(attn_out, grad_out, grad_acc, master_weight, moment_m, moment_v)


def collective_shards(n_dp, n_tensor, attn_out, grad_out, grad_acc, master_weight, moment_m, moment_v):
    entry_count = grad_out.shape[1] * attn_out.shape[1] * n_tensor
    batch_grad = lax.psum_scatter(
        lax.dot_general(
            grad_out, attn_out, (((0,), (0,)), ((), ())), preferred_element_type=jnp.float32
        ),
        "dp",
        scatter_dimension=0,
        tiled=True,
    )
    gradient = grad_acc + batch_grad
    grad_energy = lax.psum(jnp.sum(gradient * gradient), ("dp", "tensor"))
    divisor = jnp.sqrt(grad_energy / entry_count + epsilon)
    moment_new, second_new, update = lamb_moments(gradient, divisor, master_weight, moment_m, moment_v)
    squares = jnp.stack([jnp.sum(master_weight * master_weight, axis=1), jnp.sum(update * update, axis=1)])
    weight_norm, update_norm = jnp.sqrt(lax.psum(squares, "tensor"))
    return (moment_new, second_new, (weight_norm / (update_norm + epsilon))[:, None] * update)


def solution(mesh):
    n_dp, n_tensor = mesh.shape["dp"], mesh.shape["tensor"]
    fits = n_dp % 2 == 0 and 2 <= n_dp // 2 <= MAX_LINE
    shards = functools.partial(kernel_shards if fits else collective_shards, n_dp, n_tensor)
    split = P("dp", "tensor")
    in_specs = (split, P("dp", None), split, split, split, split)
    return jax.shard_map(shards, mesh=mesh, in_specs=in_specs, out_specs=(split,) * 3, check_vma=False)
```

```python
import functools

import jax
import jax.numpy as jnp
from jax import lax
from jax.experimental import pallas as pl
from jax.experimental.pallas import tpu as pltpu
from jax.sharding import PartitionSpec as P

beta_first = 0.9
beta_second = 0.999
weight_decay = 0.01
epsilon = 1e-06

MESH = pl.DeviceIdType.MESH
CHUNKS = 4
AHEAD = 4
LANES = 128
MAX_LINE = 4


def lamb_moments(gradient, divisor, weight, moment, second):
    clipped = gradient / divisor
    moment_new = beta_first * moment + (1.0 - beta_first) * clipped
    second_new = beta_second * second + (1.0 - beta_second) * clipped * clipped
    update = moment_new / (jnp.sqrt(second_new) + epsilon) + weight_decay * weight
    return (moment_new, second_new, update)


def block_order(at, line):
    right = list(range(line - 1, at, -1))
    left = list(range(0, at))
    order = []
    while right or left:
        group = []
        if right and len(right) >= len(left):
            group.append(right.pop(0))
            if left and len(left) > len(right):
                group.append(left.pop(0))
        else:
            group.append(left.pop(0))
            if right and len(right) > len(left):
                group.append(right.pop(0))
        order += [(place, chunk) for chunk in range(CHUNKS) for place in group]
    return order + [(at, chunk) for chunk in range(CHUNKS)]


def lane_sums(values):
    total = values[:, :LANES]
    for at in range(LANES, values.shape[1], LANES):
        total = total + values[:, at : at + LANES]
    return total


def row_groups(values):
    total = values[:8]
    for at in range(8, values.shape[0], 8):
        total = total + values[at : at + 8]
    return total


def lamb_kernel(
    n_dp, n_tensor, entry_count,
    attn, grad_out, grad_acc, weight, moment, second,
    grad_out_ref, divisor_out, trust_out,
    a_buf, g_buf, gt_buf, part, pair_in, from_left, from_right,
    acc_buf, w_buf, m_buf, v_buf, grad_buf, div_buf, trust_buf,
    wsum, usum, esum, tsum,
    load_sem, out_sem,
    pair_send, pair_recv, right_send, right_recv, left_send, left_recv,
    w_send, w_recv, u_send, u_recv, e_send, e_recv, t_send, t_recv,
):
    line = n_dp // 2
    dp = lax.axis_index("dp")
    tensor = lax.axis_index("tensor")
    place, side = dp // 2, dp % 2
    width = part.shape[3]

    loads = [pltpu.make_async_copy(grad_out, g_buf, load_sem.at[0])]
    for c in range(CHUNKS):
        loads.append(
            pltpu.make_async_copy(attn.at[:, pl.ds(c * width, width)], a_buf.at[c], load_sem.at[1 + c])
        )
    for i, (src, dst) in enumerate(((weight, w_buf), (grad_acc, acc_buf), (moment, m_buf), (second, v_buf))):
        loads.append(pltpu.make_async_copy(src, dst, load_sem.at[1 + CHUNKS + i]))
    for copy in loads:
        copy.start()

    dp_peer = [lax.rem(dp + k, n_dp) for k in range(n_dp)]
    tensor_peer = [lax.rem(tensor + k, n_tensor) for k in range(n_tensor)]

    barrier = pltpu.get_barrier_semaphore()
    for k in range(1, n_dp):
        pl.semaphore_signal(barrier, inc=1, device_id=(dp_peer[k], tensor), device_id_type=MESH)
    for k in range(1, n_tensor):
        pl.semaphore_signal(barrier, inc=1, device_id=(dp, tensor_peer[k]), device_id_type=MESH)

    def pair_copy(item):
        to, c = item
        i = to * CHUNKS + c
        return pltpu.make_async_remote_copy(
            src_ref=part.at[2 * to + (1 - side), c], dst_ref=pair_in.at[to, c],
            send_sem=pair_send.at[i], recv_sem=pair_recv.at[i],
            device_id=(2 * place + (1 - side), tensor), device_id_type=MESH,
        )

    def line_copy(item, step):
        to, c = item
        i = to * CHUNKS + c
        into, send, recv = (from_left, right_send, right_recv) if step > 0 else (from_right, left_send, left_recv)
        return pltpu.make_async_remote_copy(
            src_ref=part.at[2 * to + side, c], dst_ref=into.at[to, c],
            send_sem=send.at[i], recv_sem=recv.at[i],
            device_id=(dp + 2 * step, tensor), device_id_type=MESH,
        )

    def tensor_copy(k, src, dst, send, recv):
        return pltpu.make_async_remote_copy(
            src_ref=src, dst_ref=dst.at[k], send_sem=send.at[k], recv_sem=recv.at[k],
            device_id=(dp, tensor_peer[k]), device_id_type=MESH,
        )

    def dp_copy(k, src, dst, send, recv):
        return pltpu.make_async_remote_copy(
            src_ref=src, dst_ref=dst.at[k], send_sem=send.at[k], recv_sem=recv.at[k],
            device_id=(dp_peer[k], tensor), device_id_type=MESH,
        )

    loads[0].wait()
    gt_buf[...] = g_buf[...].T

    orders = [block_order(at, line) for at in range(line)]
    for c in range(CHUNKS):
        loads[1 + c].wait()
        product = jnp.dot(gt_buf[...], a_buf[c], preferred_element_type=jnp.float32)
        part[:, c] = product.reshape(n_dp, product.shape[0] // n_dp, width)
        if c == 0:
            pl.semaphore_wait(barrier, n_dp + n_tensor - 2)
        for at in range(line):
            @pl.when(place == at)
            def _(at=at, c=c):
                for item in orders[at][:AHEAD]:
                    if item[1] == c:
                        pair_copy(item).start()

    loads[1 + CHUNKS].wait()
    wsum[0] = lane_sums(jnp.square(w_buf[...]))
    w_copies = [tensor_copy(k, wsum.at[0], wsum, w_send, w_recv) for k in range(1, n_tensor)]
    for copy in w_copies:
        copy.start()
    for i in range(1, 4):
        loads[1 + CHUNKS + i].wait()

    for at in range(line):
        @pl.when(place == at)
        def _(at=at):
            order = orders[at]
            energy = jnp.zeros((8, LANES), jnp.float32)
            for i, item in enumerate(order):
                to, c = item
                pair_copy(item).wait_recv()
                if i + AHEAD < len(order):
                    pair_copy(order[i + AHEAD]).start()
                total = part[2 * to + side, c] + pair_in[to, c]
                if at > 0 and to >= at:
                    line_copy(item, 1).wait_recv()
                    total = total + from_left[to, c]
                if at < line - 1 and to <= at:
                    line_copy(item, -1).wait_recv()
                    total = total + from_right[to, c]
                if to != at:
                    part[2 * to + side, c] = total
                    line_copy(item, 1 if to > at else -1).start()
                else:
                    total = total + acc_buf[:, c * width : (c + 1) * width]
                    grad_buf[:, c * width : (c + 1) * width] = total
                    energy = energy + row_groups(lane_sums(jnp.square(total)))
            tsum[0] = energy

    outs = [
        pltpu.make_async_copy(grad_buf, grad_out_ref, out_sem.at[0]),
        pltpu.make_async_copy(div_buf, divisor_out, out_sem.at[1]),
        pltpu.make_async_copy(trust_buf, trust_out, out_sem.at[2]),
    ]
    t_copies = [tensor_copy(k, tsum.at[0], tsum, t_send, t_recv) for k in range(1, n_tensor)]
    for copy in t_copies:
        copy.start()
    outs[0].start()
    energy = tsum[0]
    for k, copy in enumerate(t_copies):
        copy.wait_recv()
        energy = energy + tsum[k + 1]
    esum[0] = energy
    e_copies = [dp_copy(k, esum.at[0], esum, e_send, e_recv) for k in range(1, n_dp)]
    for copy in e_copies:
        copy.start()
    for k, copy in enumerate(e_copies):
        copy.wait_recv()
        energy = energy + esum[k + 1]
    mean_square = jnp.sum(energy, keepdims=True) * (1.0 / entry_count)
    divisor = jnp.sqrt(mean_square + epsilon)

    div_buf[...] = jnp.broadcast_to(divisor, div_buf.shape)
    outs[1].start()
    update = lamb_moments(grad_buf[...], divisor, w_buf[...], m_buf[...], v_buf[...])[2]
    usum[0] = lane_sums(update * update)
    u_copies = [tensor_copy(k, usum.at[0], usum, u_send, u_recv) for k in range(1, n_tensor)]
    for copy in u_copies:
        copy.start()
    weight_square = wsum[0]
    for k, copy in enumerate(w_copies):
        copy.wait_recv()
        weight_square = weight_square + wsum[k + 1]
    weight_norm = jnp.sqrt(jnp.sum(weight_square, axis=1, keepdims=True))
    update_square = usum[0]
    for k, copy in enumerate(u_copies):
        copy.wait_recv()
        update_square = update_square + usum[k + 1]
    update_norm = jnp.sqrt(jnp.sum(update_square, axis=1, keepdims=True))
    trust_buf[...] = jnp.broadcast_to(weight_norm / (update_norm + epsilon), trust_buf.shape)
    outs[2].start()

    for copy in w_copies + t_copies + e_copies + u_copies:
        copy.wait_send()
    for at in range(line):
        @pl.when(place == at)
        def _(at=at):
            for item in orders[at]:
                pair_copy(item).wait_send()
                if item[0] != at:
                    line_copy(item, 1 if item[0] > at else -1).wait_send()
    for copy in outs:
        copy.wait()


def result_kernel(gradient, divisor, trust, weight, moment, second, moment_out, second_out, step_out):
    moment_new, second_new, update = lamb_moments(
        gradient[...], divisor[:1, :1], weight[...], moment[...], second[...]
    )
    moment_out[...] = moment_new
    second_out[...] = second_new
    step_out[...] = trust[:, :1] * update


def kernel_shards(n_dp, n_tensor, attn_out, grad_out, grad_acc, master_weight, moment_m, moment_v):
    tokens, columns = attn_out.shape
    rows_all = grad_out.shape[1]
    rows = rows_all // n_dp
    line = n_dp // 2
    width = columns // CHUNKS
    f32 = jnp.float32
    items = line * CHUNKS
    dma = pltpu.SemaphoreType.DMA
    whole = lambda: pltpu.VMEM((rows, columns), f32)
    out = lambda height, width: jax.ShapeDtypeStruct((height, width), f32)
    gradient, divisor, trust = pl.pallas_call(
        functools.partial(lamb_kernel, n_dp, n_tensor, rows_all * columns * n_tensor),
        out_shape=(out(rows, columns), out(8, LANES), out(rows, LANES)),
        in_specs=[pl.BlockSpec(memory_space=pltpu.HBM)] * 6,
        out_specs=[pl.BlockSpec(memory_space=pltpu.HBM)] * 3,
        scratch_shapes=[
            pltpu.VMEM((CHUNKS, tokens, width), jnp.bfloat16),
            pltpu.VMEM((tokens, rows_all), jnp.bfloat16),
            pltpu.VMEM((rows_all, tokens), jnp.bfloat16),
            pltpu.VMEM((n_dp, CHUNKS, rows, width), f32),
            pltpu.VMEM((line, CHUNKS, rows, width), f32),
            pltpu.VMEM((line, CHUNKS, rows, width), f32),
            pltpu.VMEM((line, CHUNKS, rows, width), f32),
            whole(), whole(), whole(), whole(), whole(), pltpu.VMEM((8, LANES), f32), pltpu.VMEM((rows, LANES), f32),
            pltpu.VMEM((n_tensor, rows, LANES), f32),
            pltpu.VMEM((n_tensor, rows, LANES), f32),
            pltpu.VMEM((n_dp, 8, LANES), f32),
            pltpu.VMEM((n_tensor, 8, LANES), f32),
            dma((CHUNKS + 5,)), dma((3,)),
            dma((items,)), dma((items,)), dma((items,)), dma((items,)), dma((items,)), dma((items,)),
            dma((n_tensor,)), dma((n_tensor,)), dma((n_tensor,)), dma((n_tensor,)),
            dma((n_dp,)), dma((n_dp,)), dma((n_tensor,)), dma((n_tensor,)),
        ],
        compiler_params=pltpu.CompilerParams(
            collective_id=0, has_side_effects=True, vmem_limit_bytes=56 * 2**20
        ),
        name="lamb_step",
    )(attn_out, grad_out, grad_acc, master_weight, moment_m, moment_v)
    return pl.pallas_call(
        result_kernel,
        out_shape=(out(rows, columns),) * 3,
        in_specs=[pl.BlockSpec(memory_space=pltpu.VMEM)] * 6,
        out_specs=[pl.BlockSpec(memory_space=pltpu.VMEM)] * 3,
        compiler_params=pltpu.CompilerParams(vmem_limit_bytes=8 * 2**20),
        name="results",
    )(gradient, divisor, trust, master_weight, moment_m, moment_v)


def collective_shards(n_dp, n_tensor, attn_out, grad_out, grad_acc, master_weight, moment_m, moment_v):
    entry_count = grad_out.shape[1] * attn_out.shape[1] * n_tensor
    batch_grad = lax.psum_scatter(
        lax.dot_general(
            grad_out, attn_out, (((0,), (0,)), ((), ())), preferred_element_type=jnp.float32
        ),
        "dp",
        scatter_dimension=0,
        tiled=True,
    )
    gradient = grad_acc + batch_grad
    grad_energy = lax.psum(jnp.sum(gradient * gradient), ("dp", "tensor"))
    divisor = jnp.sqrt(grad_energy / entry_count + epsilon)
    moment_new, second_new, update = lamb_moments(gradient, divisor, master_weight, moment_m, moment_v)
    squares = jnp.stack([jnp.sum(master_weight * master_weight, axis=1), jnp.sum(update * update, axis=1)])
    weight_norm, update_norm = jnp.sqrt(lax.psum(squares, "tensor"))
    return (moment_new, second_new, (weight_norm / (update_norm + epsilon))[:, None] * update)


def solution(mesh):
    n_dp, n_tensor = mesh.shape["dp"], mesh.shape["tensor"]
    fits = n_dp % 2 == 0 and 2 <= n_dp // 2 <= MAX_LINE
    shards = functools.partial(kernel_shards if fits else collective_shards, n_dp, n_tensor)
    split = P("dp", "tensor")
    in_specs = (split, P("dp", None), split, split, split, split)
    return jax.shard_map(shards, mesh=mesh, in_specs=in_specs, out_specs=(split,) * 3, check_vma=False)
```

```python
import functools

import jax
import jax.numpy as jnp
from jax import lax
from jax.experimental import pallas as pl
from jax.experimental.pallas import tpu as pltpu
from jax.sharding import PartitionSpec as P

beta_first = 0.9
beta_second = 0.999
weight_decay = 0.01
epsilon = 1e-06

MESH = pl.DeviceIdType.MESH
CHUNKS = 8
AHEAD = 8
LANES = 128
MAX_LINE = 4


def lamb_moments(gradient, divisor, weight, moment, second):
    clipped = gradient / divisor
    moment_new = beta_first * moment + (1.0 - beta_first) * clipped
    second_new = beta_second * second + (1.0 - beta_second) * clipped * clipped
    update = moment_new / (jnp.sqrt(second_new) + epsilon) + weight_decay * weight
    return (moment_new, second_new, update)


def block_order(at, line):
    right = list(range(line - 1, at, -1))
    left = list(range(0, at))
    order = []
    while right or left:
        group = []
        if right and len(right) >= len(left):
            group.append(right.pop(0))
            if left and len(left) > len(right):
                group.append(left.pop(0))
        else:
            group.append(left.pop(0))
            if right and len(right) > len(left):
                group.append(right.pop(0))
        order += [(place, chunk) for chunk in range(1, CHUNKS) for place in group]
    return order + [(at, chunk) for chunk in range(1, CHUNKS)]


def line_first_steps(at, line):
    right = [(to, 4 * at + 2 * (line - 1 - to)) for to in range(line - 1, at, -1)]
    left = [(to, 4 * (line - 1 - at) + 2 * to) for to in range(at)]
    own = max(4 * at + 2 * (line - 1 - at), 4 * (line - 1 - at) + 2 * at) + 2
    return sorted(right + left, key=lambda step: step[1]) + [(at, own)]


def lane_sums(values):
    total = values[:, :LANES]
    for at in range(LANES, values.shape[1], LANES):
        total = total + values[:, at : at + LANES]
    return total


def row_groups(values):
    total = values[:8]
    for at in range(8, values.shape[0], 8):
        total = total + values[at : at + 8]
    return total


def lamb_kernel(
    n_dp, n_tensor, entry_count,
    attn, grad_out, grad_acc, weight, moment, second,
    grad_out_ref, stats_out,
    a_buf, g_buf, gt_buf, part, pair_in, from_left, from_right,
    first, first_pair, first_left, first_right,
    acc_buf, w_buf, m_buf, v_buf, grad_buf, stats,
    wsum, usum, esum, tsum,
    load_sem, out_sem,
    pair_send, pair_recv, right_send, right_recv, left_send, left_recv,
    w_send, w_recv, u_send, u_recv, e_send, e_recv, t_send, t_recv,
):
    line = n_dp // 2
    dp = lax.axis_index("dp")
    tensor = lax.axis_index("tensor")
    place, side = dp // 2, dp % 2
    width = part.shape[3]

    loads = [pltpu.make_async_copy(grad_out, g_buf, load_sem.at[0])]
    chunk_order = [1, 0] + list(range(2, CHUNKS))
    a_loads = [
        pltpu.make_async_copy(attn.at[:, pl.ds(c * width, width)], a_buf.at[c], load_sem.at[1 + c])
        for c in chunk_order
    ]
    loads += a_loads
    for i, (src, dst) in enumerate(((weight, w_buf), (grad_acc, acc_buf), (moment, m_buf), (second, v_buf))):
        loads.append(pltpu.make_async_copy(src, dst, load_sem.at[1 + CHUNKS + i]))
    for copy in loads:
        copy.start()

    dp_peer = [lax.rem(dp + k, n_dp) for k in range(n_dp)]
    tensor_peer = [lax.rem(tensor + k, n_tensor) for k in range(n_tensor)]

    barrier = pltpu.get_barrier_semaphore()
    for k in range(1, n_dp):
        pl.semaphore_signal(barrier, inc=1, device_id=(dp_peer[k], tensor), device_id_type=MESH)
    for k in range(1, n_tensor):
        pl.semaphore_signal(barrier, inc=1, device_id=(dp, tensor_peer[k]), device_id_type=MESH)

    def pair_copy(item):
        to, c = item
        i = to * CHUNKS + c
        return pltpu.make_async_remote_copy(
            src_ref=part.at[2 * to + (1 - side), c], dst_ref=pair_in.at[to, c],
            send_sem=pair_send.at[i], recv_sem=pair_recv.at[i],
            device_id=(2 * place + (1 - side), tensor), device_id_type=MESH,
        )

    def line_copy(item, step):
        to, c = item
        i = to * CHUNKS + c
        into, send, recv = (from_left, right_send, right_recv) if step > 0 else (from_right, left_send, left_recv)
        return pltpu.make_async_remote_copy(
            src_ref=part.at[2 * to + side, c], dst_ref=into.at[to, c],
            send_sem=send.at[i], recv_sem=recv.at[i],
            device_id=(dp + 2 * step, tensor), device_id_type=MESH,
        )

    def first_line_copy(to, step):
        i = to * CHUNKS
        into, send, recv = (first_left, right_send, right_recv) if step > 0 else (first_right, left_send, left_recv)
        return pltpu.make_async_remote_copy(
            src_ref=first.at[to], dst_ref=into.at[to], send_sem=send.at[i], recv_sem=recv.at[i],
            device_id=(dp + 2 * step, tensor), device_id_type=MESH,
        )

    def first_pair_copy(at):
        return pltpu.make_async_remote_copy(
            src_ref=first.at[at, 1 - side], dst_ref=first_pair,
            send_sem=pair_send.at[at * CHUNKS], recv_sem=pair_recv.at[at * CHUNKS],
            device_id=(2 * place + (1 - side), tensor), device_id_type=MESH,
        )

    def first_step(at, to):
        if to == at:
            total = first[at]
            if at > 0:
                first_line_copy(at, 1).wait_recv()
                total = total + first_left[at]
            if at < line - 1:
                first_line_copy(at, -1).wait_recv()
                total = total + first_right[at]
            first[at] = total
            first_pair_copy(at).start()
            return
        step = 1 if to > at else -1
        if step > 0 and at > 0:
            first_line_copy(to, 1).wait_recv()
            first[to] = first[to] + first_left[to]
        if step < 0 and at < line - 1:
            first_line_copy(to, -1).wait_recv()
            first[to] = first[to] + first_right[to]
        first_line_copy(to, step).start()

    def tensor_copy(k, src, dst, send, recv):
        return pltpu.make_async_remote_copy(
            src_ref=src, dst_ref=dst.at[k], send_sem=send.at[k], recv_sem=recv.at[k],
            device_id=(dp, tensor_peer[k]), device_id_type=MESH,
        )

    def dp_copy(k, src, dst, send, recv):
        return pltpu.make_async_remote_copy(
            src_ref=src, dst_ref=dst.at[k], send_sem=send.at[k], recv_sem=recv.at[k],
            device_id=(dp_peer[k], tensor), device_id_type=MESH,
        )

    loads[0].wait()
    gt_buf[...] = g_buf[...].T

    orders = [block_order(at, line) for at in range(line)]
    for n, c in enumerate(chunk_order):
        a_loads[n].wait()
        product = jnp.dot(gt_buf[...], a_buf[c], preferred_element_type=jnp.float32)
        if c == 0:
            first[...] = product.reshape(first.shape)
        else:
            part[:, c] = product.reshape(n_dp, product.shape[0] // n_dp, width)
        if n == 0:
            pl.semaphore_wait(barrier, n_dp + n_tensor - 2)
        for at in range(line):
            @pl.when(place == at)
            def _(at=at, c=c):
                for item in orders[at][:AHEAD]:
                    if item[1] == c:
                        pair_copy(item).start()
                if c == 0 and at in (0, line - 1):
                    for to, _ in line_first_steps(at, line)[:-1]:
                        first_step(at, to)

    loads[1 + CHUNKS].wait()
    wsum[0] = lane_sums(jnp.square(w_buf[...]))
    w_copies = [tensor_copy(k, wsum.at[0], wsum, w_send, w_recv) for k in range(1, n_tensor)]
    for copy in w_copies:
        copy.start()
    for i in range(1, 4):
        loads[1 + CHUNKS + i].wait()

    for at in range(line):
        @pl.when(place == at)
        def _(at=at):
            order = orders[at]
            energy = jnp.zeros((8, LANES), jnp.float32)
            early = line_first_steps(at, line)
            if at in (0, line - 1):
                early = early[-1:]
            for i, item in enumerate(order):
                to, c = item
                for early_to, when in early:
                    if when == i:
                        first_step(at, early_to)
                if i == len(order) - 4:
                    first_pair_copy(at).wait_recv()
                    total = first[at, side] + first_pair[...] + acc_buf[:, :width]
                    grad_buf[:, :width] = total
                    energy = energy + row_groups(lane_sums(jnp.square(total)))
                pair_copy(item).wait_recv()
                if i + AHEAD < len(order):
                    pair_copy(order[i + AHEAD]).start()
                total = part[2 * to + side, c] + pair_in[to, c]
                if at > 0 and to >= at:
                    line_copy(item, 1).wait_recv()
                    total = total + from_left[to, c]
                if at < line - 1 and to <= at:
                    line_copy(item, -1).wait_recv()
                    total = total + from_right[to, c]
                if to != at:
                    part[2 * to + side, c] = total
                    line_copy(item, 1 if to > at else -1).start()
                else:
                    total = total + acc_buf[:, c * width : (c + 1) * width]
                    grad_buf[:, c * width : (c + 1) * width] = total
                    energy = energy + row_groups(lane_sums(jnp.square(total)))
            tsum[0] = energy

    outs = [
        pltpu.make_async_copy(grad_buf, grad_out_ref, out_sem.at[0]),
        pltpu.make_async_copy(stats, stats_out, out_sem.at[1]),
    ]
    t_copies = [tensor_copy(k, tsum.at[0], tsum, t_send, t_recv) for k in range(1, n_tensor)]
    for copy in t_copies:
        copy.start()
    outs[0].start()
    energy = tsum[0]
    for k, copy in enumerate(t_copies):
        copy.wait_recv()
        energy = energy + tsum[k + 1]
    esum[0] = energy
    e_copies = [dp_copy(k, esum.at[0], esum, e_send, e_recv) for k in range(1, n_dp)]
    for copy in e_copies:
        copy.start()
    for k, copy in enumerate(e_copies):
        copy.wait_recv()
        energy = energy + esum[k + 1]
    mean_square = jnp.sum(energy, keepdims=True) * (1.0 / entry_count)
    divisor = jnp.sqrt(mean_square + epsilon)

    stats[:8] = jnp.broadcast_to(divisor, (8, LANES))
    update = lamb_moments(grad_buf[...], divisor, w_buf[...], m_buf[...], v_buf[...])[2]
    usum[0] = lane_sums(update * update)
    u_copies = [tensor_copy(k, usum.at[0], usum, u_send, u_recv) for k in range(1, n_tensor)]
    for copy in u_copies:
        copy.start()
    weight_square = wsum[0]
    for k, copy in enumerate(w_copies):
        copy.wait_recv()
        weight_square = weight_square + wsum[k + 1]
    weight_norm = jnp.sqrt(jnp.sum(weight_square, axis=1, keepdims=True))
    update_square = usum[0]
    for k, copy in enumerate(u_copies):
        copy.wait_recv()
        update_square = update_square + usum[k + 1]
    update_norm = jnp.sqrt(jnp.sum(update_square, axis=1, keepdims=True))
    stats[8:] = jnp.broadcast_to(weight_norm / (update_norm + epsilon), (stats.shape[0] - 8, LANES))
    outs[1].start()

    for copy in w_copies + t_copies + e_copies + u_copies:
        copy.wait_send()
    for at in range(line):
        @pl.when(place == at)
        def _(at=at):
            first_pair_copy(at).wait_send()
            for to in range(line):
                if to != at:
                    first_line_copy(to, 1 if to > at else -1).wait_send()
            for item in orders[at]:
                pair_copy(item).wait_send()
                if item[0] != at:
                    line_copy(item, 1 if item[0] > at else -1).wait_send()
    for copy in outs:
        copy.wait()


def result_kernel(*refs):
    sources, (moment_out, second_out, step_out), buffers, sem = refs[:5], refs[5:8], refs[8:13], refs[13]
    loads = [pltpu.make_async_copy(src, dst, sem.at[i]) for i, (src, dst) in enumerate(zip(sources, buffers))]
    for copy in loads:
        copy.start()
    for copy in loads:
        copy.wait()
    gradient, stats, weight, moment, second = buffers
    moment_new, second_new, update = lamb_moments(
        gradient[...], stats[:1, :1], weight[...], moment[...], second[...]
    )
    moment_out[...] = moment_new
    second_out[...] = second_new
    step_out[...] = stats[8:, :1] * update


def kernel_shards(n_dp, n_tensor, attn_out, grad_out, grad_acc, master_weight, moment_m, moment_v):
    tokens, columns = attn_out.shape
    rows_all = grad_out.shape[1]
    rows = rows_all // n_dp
    line = n_dp // 2
    width = columns // CHUNKS
    f32 = jnp.float32
    items = line * CHUNKS
    dma = pltpu.SemaphoreType.DMA
    whole = lambda: pltpu.VMEM((rows, columns), f32)
    out = lambda height, width: jax.ShapeDtypeStruct((height, width), f32)
    gradient, stats = pl.pallas_call(
        functools.partial(lamb_kernel, n_dp, n_tensor, rows_all * columns * n_tensor),
        out_shape=(out(rows, columns), out(8 + rows, LANES)),
        in_specs=[pl.BlockSpec(memory_space=pltpu.HBM)] * 6,
        out_specs=[pl.BlockSpec(memory_space=pltpu.HBM)] * 2,
        scratch_shapes=[
            pltpu.VMEM((CHUNKS, tokens, width), jnp.bfloat16),
            pltpu.VMEM((tokens, rows_all), jnp.bfloat16),
            pltpu.VMEM((rows_all, tokens), jnp.bfloat16),
            pltpu.VMEM((n_dp, CHUNKS, rows, width), f32),
            pltpu.VMEM((line, CHUNKS, rows, width), f32),
            pltpu.VMEM((line, CHUNKS, rows, width), f32),
            pltpu.VMEM((line, CHUNKS, rows, width), f32),
            pltpu.VMEM((line, 2, rows, width), f32),
            pltpu.VMEM((rows, width), f32),
            pltpu.VMEM((line, 2, rows, width), f32),
            pltpu.VMEM((line, 2, rows, width), f32),
            whole(), whole(), whole(), whole(), whole(), pltpu.VMEM((8 + rows, LANES), f32),
            pltpu.VMEM((n_tensor, rows, LANES), f32),
            pltpu.VMEM((n_tensor, rows, LANES), f32),
            pltpu.VMEM((n_dp, 8, LANES), f32),
            pltpu.VMEM((n_tensor, 8, LANES), f32),
            dma((CHUNKS + 5,)), dma((2,)),
            dma((items,)), dma((items,)), dma((items,)), dma((items,)), dma((items,)), dma((items,)),
            dma((n_tensor,)), dma((n_tensor,)), dma((n_tensor,)), dma((n_tensor,)),
            dma((n_dp,)), dma((n_dp,)), dma((n_tensor,)), dma((n_tensor,)),
        ],
        compiler_params=pltpu.CompilerParams(
            collective_id=0, has_side_effects=True, vmem_limit_bytes=56 * 2**20
        ),
        name="lamb_step",
    )(attn_out, grad_out, grad_acc, master_weight, moment_m, moment_v)
    return pl.pallas_call(
        result_kernel,
        out_shape=(out(rows, columns),) * 3,
        in_specs=[pl.BlockSpec(memory_space=pltpu.HBM)] * 5,
        out_specs=[pl.BlockSpec(memory_space=pltpu.VMEM)] * 3,
        scratch_shapes=[whole(), pltpu.VMEM((8 + rows, LANES), f32), whole(), whole(), whole(), dma((5,))],
        compiler_params=pltpu.CompilerParams(vmem_limit_bytes=56 * 2**20),
        name="results",
    )(gradient, stats, master_weight, moment_m, moment_v)


def collective_shards(n_dp, n_tensor, attn_out, grad_out, grad_acc, master_weight, moment_m, moment_v):
    entry_count = grad_out.shape[1] * attn_out.shape[1] * n_tensor
    batch_grad = lax.psum_scatter(
        lax.dot_general(
            grad_out, attn_out, (((0,), (0,)), ((), ())), preferred_element_type=jnp.float32
        ),
        "dp",
        scatter_dimension=0,
        tiled=True,
    )
    gradient = grad_acc + batch_grad
    grad_energy = lax.psum(jnp.sum(gradient * gradient), ("dp", "tensor"))
    divisor = jnp.sqrt(grad_energy / entry_count + epsilon)
    moment_new, second_new, update = lamb_moments(gradient, divisor, master_weight, moment_m, moment_v)
    squares = jnp.stack([jnp.sum(master_weight * master_weight, axis=1), jnp.sum(update * update, axis=1)])
    weight_norm, update_norm = jnp.sqrt(lax.psum(squares, "tensor"))
    return (moment_new, second_new, (weight_norm / (update_norm + epsilon))[:, None] * update)


def solution(mesh):
    n_dp, n_tensor = mesh.shape["dp"], mesh.shape["tensor"]
    fits = n_dp % 2 == 0 and 2 <= n_dp // 2 <= MAX_LINE
    shards = functools.partial(kernel_shards if fits else collective_shards, n_dp, n_tensor)
    split = P("dp", "tensor")
    in_specs = (split, P("dp", None), split, split, split, split)
    return jax.shard_map(shards, mesh=mesh, in_specs=in_specs, out_specs=(split,) * 3, check_vma=False)
```
